256 devices in a mesh: dp: 16 (over x, y), mp: 16 (over z, core).
Axes of the slice: x: 4, y: 4, z: 8, core: 2. Of those that a mesh axis runs over, the one named last changes fastest.
Arguments:
- hidden_state: bfloat16 [256, 8192], P('dp'), may hold values from -60 to 60, as said below
- norm_gain: bfloat16 [8192], replicated, may hold values from 0.5 to 1.5
- critic_weight: bfloat16 [8192, 65536], P(None, ('dp', 'mp')), may hold values from -8 to 8
- policy_weight: bfloat16 [8192, 65536], P(None, ('dp', 'mp')), may hold values from -8 to 8
- value_weight: bfloat16 [8192], replicated, may hold values from -0.0625 to 0.0625
- actions: int32 [256], replicated, may hold values from 0 to 65535, as said below
- rewards: int32 [256], replicated, may hold values from -4 to 4
- done_flags: int32 [256], replicated, may hold values 0 or 1
- pad_mask: int32 [256], replicated, may hold values 0 or 1
Outputs:
- grad_hidden: bfloat16 [256, 8192], P(('dp', 'mp'))
- grad_gain: float32 [8192], replicated
- grad_critic: bfloat16 [8192, 65536], P(None, ('dp', 'mp'))
- grad_value: float32 [8192], replicated
The draws below stay inside these ranges and needn't reach their ends.
Inputs may be any that keep to these rules, and one draw needn't show every extreme that they name: `hidden_state`: hidden states of the trunk. `actions`: about half of the tokens, chosen at random, take an id from the block of 4096 ids that lies half the vocabulary away from the block at the token's own relative position (token t's block is t * 65536 // 4096 // 256); the others take any id.
All inputs are finite; a program needn't handle non-finite values.
Results may differ from the reference program's by a relative error of at most 0.0015.
The reference program's roundings to bfloat16 on the way (of `normed`, `critic_grad` and `policy_grad`) count: a program that leaves them out, or rounds other values in their place, can miss the bound.
Values may be sent and summed in bfloat16 or wider, within the bound.
No kernel may reach another device: no remote copies, remote signals or barrier semaphores. Data moves between devices by JAX's collectives and lax.ppermute only.
A program may use at most 128 MiB of HBM per device.

```python
import math
import jax
import jax.numpy as jnp
from jax import lax

D = 8192
VOC_DEV = 4096
TOKENS = 256
VOCAB = 65536


def shared_parts(key):
    halves = jax.random.uniform(jax.random.fold_in(key, 92), (D // 2,), jnp.float32, 0.5, 1.5)
    mean_dir = jnp.repeat(halves, 2)
    picked = jax.random.bernoulli(jax.random.fold_in(key, 93), 0.5, (D // 2,))
    signs = jnp.where(picked, 1.0, -1.0).astype(jnp.float32)
    crossing = jnp.stack([signs, -signs], axis=1).reshape(D)
    return (mean_dir, crossing)


def shape_block(matrix, detail, mean_dir, crossing, offset_scale):
    block = (jnp.arange(VOCAB) % 32 == 5)[None, :]
    special = 0.33 * detail + offset_scale * mean_dir[:, None] / D + 6.0 * crossing[:, None] / math.sqrt(D)
    return jnp.where(block, special, matrix)


def draw_hidden_state(key, part):
    mean_dir, crossing = shared_parts(key)
    key = jax.random.fold_in(key, 1)
    first, second, third = jax.random.split(key, 3)
    ramp = 3.0 ** (jnp.arange(D, dtype=jnp.float32) / D)
    column_scale = jnp.exp(jax.random.uniform(second, (1, D), jnp.float32, math.log(0.3), math.log(3.0)))
    row_scale = jnp.exp(jax.random.uniform(third, (TOKENS, 1), jnp.float32, math.log(0.1), math.log(1.0)))
    noise = jnp.clip(jax.random.normal(first, (TOKENS, D), jnp.float32), -6.0, 6.0)
    result = (noise * column_scale * ramp[None, :] + 1.8 * mean_dir[None, :]) * row_scale
    return result.astype(jnp.bfloat16)


def draw_critic_weight(key, part):
    mean_dir, crossing = shared_parts(key)
    key = jax.random.fold_in(key, 2)
    spread = 3.0 / math.sqrt(D)
    matrix = jnp.clip(jax.random.normal(key, (D, VOCAB), jnp.float32), -6.0, 6.0) * spread
    matrix = shape_block(matrix, matrix, mean_dir, crossing, 12.5)
    return matrix.astype(jnp.bfloat16)


def draw_policy_weight(key, part):
    mean_dir, crossing = shared_parts(key)
    key = jax.random.fold_in(key, 3)
    spread = 3.0 / math.sqrt(D)
    matrix = jnp.clip(jax.random.normal(key, (D, VOCAB), jnp.float32), -6.0, 6.0) * spread
    matrix = shape_block(matrix, matrix, mean_dir, crossing, 12.5)
    return matrix.astype(jnp.bfloat16)


def draw_actions(key, part):
    key = jax.random.fold_in(key, 4)
    first, second, third = jax.random.split(key, 3)
    shard_count = VOCAB // VOC_DEV
    position = jnp.arange(TOKENS, dtype=jnp.int32)
    home_block = position * shard_count // TOKENS
    far_block = (home_block + shard_count // 2) % shard_count
    far_ids = far_block * VOC_DEV + jax.random.randint(first, (TOKENS,), 0, VOC_DEV, jnp.int32)
    any_ids = jax.random.randint(second, (TOKENS,), 0, VOCAB, jnp.int32)
    coin = jax.random.randint(third, (TOKENS,), 0, 2, jnp.int32)
    return jnp.where(coin == 1, far_ids, any_ids).astype(jnp.int32)


def set_ends(values, key, least, high):
    longest = values.shape.index(max(values.shape))
    spots = []
    for shift in (0, 1):
        where = [jax.random.randint(jax.random.fold_in(key, axis), (), 0, length) for axis, length in enumerate(values.shape)]
        where[longest] = (where[longest] + shift) % values.shape[longest]
        spots.append(tuple(where))
    return values.at[spots[0]].set(least).at[spots[1]].set(high)


def scatter_about(own_key, extent, scale, limit, kind=jnp.bfloat16):
    drawn = jax.random.normal(own_key, extent, jnp.float32) * scale
    return jnp.minimum(jnp.maximum(drawn, -limit), limit).astype(kind)


def setup_inputs(seed: int = 0) -> dict:
    key_list = jax.random.split(jax.random.key(seed), 10)
    return {
        "hidden_state": draw_hidden_state(jax.random.fold_in(key_list[9], 71), 0),
        "norm_gain": jnp.clip(1.0 + 0.1 * jax.random.normal(key_list[1], (D,), jnp.float32), 0.5, 1.5).astype(jnp.bfloat16),
        "critic_weight": draw_critic_weight(jax.random.fold_in(key_list[9], 71), 0),
        "policy_weight": draw_policy_weight(jax.random.fold_in(key_list[9], 71), 0),
        "value_weight": scatter_about(key_list[4], (D,), D ** -0.5, 0.0625),
        "actions": draw_actions(jax.random.fold_in(key_list[9], 71), 0),
        "rewards": set_ends(jax.random.randint(key_list[6], (TOKENS,), -4, 5), jax.random.fold_in(key_list[6], 1), -4, 4).astype(jnp.int32),
        "done_flags": set_ends((jax.random.randint(key_list[7], (TOKENS,), 0, 8) < 1).astype(jnp.int32), jax.random.fold_in(key_list[7], 1), 0, 1),
        "pad_mask": set_ends((jax.random.randint(key_list[8], (TOKENS,), 0, 8) < 7).astype(jnp.int32), jax.random.fold_in(key_list[8], 1), 0, 1),
    }


discount = 0.99
expectile = 0.7
conservative = 0.5
reward_step = 0.5
epsilon = 1e-05

def softmax_rows(logits):
    row_max = lax.optimization_barrier(jnp.max(logits, axis=1, keepdims=True))
    shifted = jnp.exp(logits - row_max)
    return shifted / lax.optimization_barrier(jnp.sum(shifted, axis=1, keepdims=True))

def contract_rows(left_side, right_side):
    return lax.dot_general(left_side, right_side, (((1,), (1,)), ((), ())), preferred_element_type=jnp.float32)

def reference(hidden_state, norm_gain, critic_weight, policy_weight, value_weight, actions, rewards, done_flags, pad_mask):
    state_float = hidden_state.astype(jnp.float32)
    row_inverse = lax.rsqrt(lax.optimization_barrier(jnp.mean(state_float * state_float, axis=1)) + epsilon)
    unit_state = state_float * row_inverse[:, None]
    gain_float = norm_gain.astype(jnp.float32)
    normed = (unit_state * gain_float[None, :]).astype(jnp.bfloat16)
    critic_logits = jnp.dot(normed, critic_weight, preferred_element_type=jnp.float32)
    policy_logits = jnp.dot(normed, policy_weight, preferred_element_type=jnp.float32)
    values = jnp.dot(normed, value_weight, preferred_element_type=jnp.float32)
    critic_probs = softmax_rows(critic_logits)
    policy_probs = softmax_rows(policy_logits)
    columns = jnp.arange(critic_logits.shape[1], dtype=jnp.int32)
    chosen = (actions[:, None] == columns[None, :]).astype(jnp.float32)
    critic_taken = lax.optimization_barrier(jnp.sum(critic_logits * chosen, axis=1))
    next_values = jnp.concatenate([values[1:], jnp.zeros((1,), jnp.float32)])
    target = reward_step * rewards.astype(jnp.float32) + discount * (1.0 - done_flags.astype(jnp.float32)) * next_values
    live_mask = pad_mask.astype(jnp.float32)
    advantage = critic_taken - values
    weights = jnp.where(advantage >= 0.0, expectile, 1.0 - expectile)
    value_coef = live_mask * -2.0 * weights * advantage
    critic_coef = live_mask * (2.0 * (critic_taken - target) - conservative)
    critic_grad = (conservative * live_mask[:, None] * critic_probs + critic_coef[:, None] * chosen).astype(jnp.bfloat16)
    policy_grad = (live_mask[:, None] * (policy_probs - chosen)).astype(jnp.bfloat16)
    grad_critic = lax.dot_general(normed, critic_grad, (((0,), (0,)), ((), ())), preferred_element_type=jnp.float32).astype(jnp.bfloat16)
    grad_value = jnp.dot(value_coef, normed, precision=lax.Precision.HIGHEST, preferred_element_type=jnp.float32)
    normed_grad = contract_rows(critic_grad, critic_weight) + contract_rows(policy_grad, policy_weight)
    normed_grad = normed_grad + value_coef[:, None] * value_weight.astype(jnp.float32)[None, :]
    scaled = normed_grad * gain_float[None, :]
    row_dot = lax.optimization_barrier(jnp.sum(scaled * unit_state, axis=1))
    grad_hidden = (row_inverse[:, None] * (scaled - unit_state * row_dot[:, None] / D)).astype(jnp.bfloat16)
    grad_gain = lax.optimization_barrier(jnp.sum(normed_grad * unit_state, axis=0))
    return (grad_hidden, grad_gain, grad_critic, grad_value)
```

```python
import jax
import jax.numpy as jnp
from jax import lax
from jax.sharding import PartitionSpec as P

D = 8192
HALF = D // 2


discount = 0.99
expectile = 0.7
conservative = 0.5
reward_step = 0.5
epsilon = 1e-05
weight_limit = 8.0


def contract_rows(left_side, right_side):
    return lax.dot_general(
        left_side, right_side, (((1,), (1,)), ((), ())), preferred_element_type=jnp.float32
    )


def contract_tokens(left_side, right_side):
    return lax.dot_general(
        left_side, right_side, (((0,), (0,)), ((), ())), preferred_element_type=jnp.float32
    )


def merge_totals(tops, totals, taken):
    top = jnp.max(tops, axis=0)
    return top, jnp.sum(totals * jnp.exp(tops - top[None]), axis=0), jnp.sum(taken, axis=0)


def body(
    hidden_state,
    norm_gain,
    critic_weight,
    policy_weight,
    value_weight,
    actions,
    rewards,
    done_flags,
    pad_mask,
):
    dp_size = lax.axis_size("dp")
    mp_size = lax.axis_size("mp")
    chip_count = mp_size // 2
    dp_index = lax.axis_index("dp")
    mp_index = lax.axis_index("mp")
    core = mp_index % 2
    core_swap = [(i, i ^ 1) for i in range(mp_size)]
    chip_groups = [[c + 2 * k for k in range(chip_count)] for c in range(2)]
    block_rows = hidden_state.shape[0]
    tokens = block_rows * dp_size

    def swap(array):
        return lax.ppermute(array, "mp", core_swap)

    def spread(array, axis, size, groups=None):
        copies = jnp.broadcast_to(array[None], (size,) + array.shape)
        return lax.all_to_all(copies, axis, 0, 0, axis_index_groups=groups)

    def half_rows(array, which):
        return lax.dynamic_slice_in_dim(array, which * HALF, HALF, 0)

    state_float = hidden_state.astype(jnp.float32)
    row_inverse = lax.rsqrt(jnp.mean(state_float * state_float, axis=1) + epsilon)
    unit_state = state_float * row_inverse[:, None]
    gain_float = norm_gain.astype(jnp.float32)
    normed_own = (unit_state * gain_float[None, :]).astype(jnp.bfloat16)

    with jax.named_scope("gather"):
        normed_half = lax.dynamic_slice_in_dim(normed_own, core * HALF, HALF, 1)
        mine = spread(normed_half, "dp", dp_size).reshape(tokens, HALF)
        other = swap(mine)

    with jax.named_scope("logits"):
        value_float = value_weight
        critic_mine, critic_other = half_rows(critic_weight, core), half_rows(critic_weight, 1 - core)
        policy_mine, policy_other = half_rows(policy_weight, core), half_rows(policy_weight, 1 - core)
        value_mine, value_other = half_rows(value_float, core), half_rows(value_float, 1 - core)

        def project(weight_mine, weight_other):
            return jnp.dot(mine, weight_mine, preferred_element_type=jnp.float32) + jnp.dot(
                other, weight_other, preferred_element_type=jnp.float32
            )

        critic_logits = project(critic_mine, critic_other)
        policy_logits = project(policy_mine, policy_other)
        values = project(value_mine, value_other)

    vocab_width = critic_weight.shape[1]
    block_index = dp_index * mp_size + mp_index
    columns = block_index * vocab_width + jnp.arange(vocab_width, dtype=jnp.int32)
    chosen = (actions[:, None] == columns[None, :]).astype(jnp.float32)

    with jax.named_scope("totals"):
        tops = jnp.stack([jnp.max(critic_logits, axis=1), jnp.max(policy_logits, axis=1)])
        totals = jnp.stack(
            [
                jnp.sum(jnp.exp(critic_logits - tops[0][:, None]), axis=1),
                jnp.sum(jnp.exp(policy_logits - tops[1][:, None]), axis=1),
            ]
        )
        taken = jnp.sum(critic_logits * chosen, axis=1)
        packed = jnp.concatenate([tops, totals, taken[None]], axis=0)

        def merge(parts):
            top, total, take = merge_totals(parts[:, 0:2], parts[:, 2:4], parts[:, 4])
            return jnp.concatenate([top, total, take[None]], axis=0)

        packed = merge(jnp.stack([packed, swap(packed)]))
        packed = merge(spread(packed, "mp", chip_count, chip_groups))
        packed = merge(spread(packed, "dp", dp_size))
        critic_max, policy_max, critic_total, policy_total, critic_taken = packed

    critic_probs = jnp.exp(critic_logits - critic_max[:, None]) / critic_total[:, None]
    policy_probs = jnp.exp(policy_logits - policy_max[:, None]) / policy_total[:, None]
    next_values = jnp.concatenate([values[1:], jnp.zeros((1,), jnp.float32)])
    target = (
        reward_step * rewards.astype(jnp.float32)
        + discount * (1.0 - done_flags.astype(jnp.float32)) * next_values
    )
    live_mask = pad_mask.astype(jnp.float32)
    advantage = critic_taken - values
    weights = jnp.where(advantage >= 0.0, expectile, 1.0 - expectile)
    value_coef = live_mask * -2.0 * weights * advantage
    critic_coef = live_mask * (2.0 * (critic_taken - target) - conservative)
    critic_grad = (
        conservative * live_mask[:, None] * critic_probs + critic_coef[:, None] * chosen
    ).astype(jnp.bfloat16)
    policy_grad = (live_mask[:, None] * (policy_probs - chosen)).astype(jnp.bfloat16)

    bound = 2.5 + jnp.abs(critic_coef)
    send_scale = (4.0 * 8192.0 / weight_limit) / bound
    back_scale = bound * (weight_limit / (4.0 * 8192.0))

    with jax.named_scope("reduce"):
        part_other = contract_rows(critic_grad, critic_other) + contract_rows(
            policy_grad, policy_other
        )
        arrived = swap((part_other * send_scale[:, None]).astype(jnp.float16))
        part_mine = contract_rows(critic_grad, critic_mine) + contract_rows(
            policy_grad, policy_mine
        )
        chip_part = (
            part_mine * send_scale[:, None] + arrived.astype(jnp.float32)
        ).astype(jnp.float16)
        chip_part = lax.all_to_all(chip_part.reshape(dp_size, block_rows, HALF), "dp", 0, 0)
        block_back = lax.dynamic_slice_in_dim(back_scale, dp_index * block_rows, block_rows, 0)
        block_coef = lax.dynamic_slice_in_dim(value_coef, dp_index * block_rows, block_rows, 0)
        block_part = jnp.sum(chip_part.astype(jnp.float32), axis=0) * block_back[:, None]
        unit_half = lax.dynamic_slice_in_dim(unit_state, core * HALF, HALF, 1)
        gain_part = jnp.sum(block_part * unit_half, axis=0)
        rows_out = jnp.concatenate(
            [
                block_part.reshape(chip_count, 2, HALF),
                jnp.broadcast_to(gain_part[None, None], (chip_count, 1, HALF)),
            ],
            axis=1,
        )
        rows_in = jnp.sum(
            lax.all_to_all(rows_out, "mp", 0, 0, axis_index_groups=chip_groups), axis=0
        )

    with jax.named_scope("gain"):
        value_half = value_mine.astype(jnp.float32)
        gain_block = rows_in[2] + value_half * jnp.sum(block_coef[:, None] * unit_half, axis=0)
        gain_mine = jnp.sum(spread(gain_block, "dp", dp_size), axis=0)
        gain_other = swap(gain_mine)
        first_core = core == 0
        grad_gain = jnp.concatenate(
            [
                jnp.where(first_core, gain_mine, gain_other),
                jnp.where(first_core, gain_other, gain_mine),
            ]
        )

    with jax.named_scope("hidden"):
        own_half = jnp.where(first_core, rows_in[0], rows_in[1])
        far_half = swap(jnp.where(first_core, rows_in[1], rows_in[0]))
        own_row = jnp.concatenate(
            [jnp.where(first_core, own_half, far_half), jnp.where(first_core, far_half, own_half)]
        )[None]
        own_coef = lax.dynamic_slice_in_dim(value_coef, block_index, 1, 0)
        own_unit = lax.dynamic_slice_in_dim(unit_state, mp_index, 1, 0)
        own_inverse = lax.dynamic_slice_in_dim(row_inverse, mp_index, 1, 0)
        normed_grad = own_row + own_coef[:, None] * value_weight.astype(jnp.float32)[None, :]
        scaled = normed_grad * gain_float[None, :]
        row_dot = jnp.sum(scaled * own_unit, axis=1)
        grad_hidden = (own_inverse[:, None] * (scaled - own_unit * row_dot[:, None] / D)).astype(
            jnp.bfloat16
        )

    with jax.named_scope("weights"):
        normed = jnp.concatenate(
            [jnp.where(first_core, mine, other), jnp.where(first_core, other, mine)], axis=1
        )
        grad_critic = contract_tokens(normed, critic_grad).astype(jnp.bfloat16)
        grad_value = jnp.sum(value_coef[:, None] * normed.astype(jnp.float32), axis=0)
    return (grad_hidden, grad_gain, grad_critic, grad_value)


def solution(mesh):
    placed = (
        P("dp", None),
        P(),
        P(None, ("dp", "mp")),
        P(None, ("dp", "mp")),
        P(),
        P(),
        P(),
        P(),
        P(),
    )
    return jax.shard_map(
        body,
        mesh=mesh,
        in_specs=placed,
        out_specs=(P(("dp", "mp"), None), P(), P(None, ("dp", "mp")), P()),
        check_vma=False,
    )
```

```python
import functools
import math

import jax
import jax.numpy as jnp
from jax import lax
from jax.experimental import pallas as pl
from jax.experimental.pallas import tpu as pltpu
from jax.sharding import PartitionSpec as P

D = 8192
HALF = D // 2
LANES = 128
TILES = HALF // LANES
CHUNK_TILES = 8
CHUNK = CHUNK_TILES * LANES
CHUNKS = TILES // CHUNK_TILES


discount = 0.99
expectile = 0.7
conservative = 0.5
reward_step = 0.5
epsilon = 1e-05
unit_limit = 91.0
half_limit = 32768.0

f32 = jnp.float32
bf16 = jnp.bfloat16
f16 = jnp.float16

roomy = pltpu.CompilerParams(vmem_limit_bytes=16 * 1024 * 1024)


def whole(shape):
    return pl.BlockSpec(shape, lambda *_: (0,) * len(shape))


def to_columns(rows):
    tokens = rows.shape[1]
    filled = jnp.concatenate([rows, jnp.zeros((LANES - rows.shape[0], tokens), f32)], axis=0)
    return jnp.transpose(filled)


def lane_pack(columns):
    tokens = columns[0].shape[0]
    lane = lax.broadcasted_iota(jnp.int32, (tokens, LANES), 1)
    packed = jnp.zeros((tokens, LANES), f32)
    for k, column in enumerate(columns):
        packed = jnp.where(lane == k, column, packed)
    return packed


def inverse_column(half, tile_ref):
    parts = gathered_tile(half, tile_ref, 0)
    return parts[:, 0:1] + parts[:, 1:2] + parts[:, 2:3]


def gathered_place(half, group, side):
    x, y = divmod(group, side)
    return jnp.where(half == 0, y * side + x, x * side + y)


def reduced_place(half, group, side):
    x, y = divmod(group, side)
    return jnp.where(half == 0, x * side + y, y * side + x)


def gathered_tile(half, state_ref, tile):
    groups = state_ref.shape[0]
    side = math.isqrt(groups)
    return jnp.concatenate(
        [
            state_ref[gathered_place(half, group, side), tile].astype(f32)
            for group in range(groups)
        ],
        axis=0,
    )


def normed_tile(half, state_ref, tile, inverse, gain_ref):
    gain = gain_ref[:, tile * LANES : (tile + 1) * LANES].astype(f32)
    unit = gathered_tile(half, state_ref, tile) * inverse
    return (unit * gain).astype(bf16)


def norm_kernel(core_ref, state_ref, half_ref, out_ref):
    state = state_ref[...].astype(f32)
    mean = jnp.sum(state * state, axis=1, keepdims=True) / D
    inverse = lax.rsqrt(mean + epsilon)
    high = inverse.astype(bf16).astype(f32)
    middle = (inverse - high).astype(bf16).astype(f32)
    low = inverse - high - middle
    packed = lane_pack([high, middle, low]).astype(bf16)
    copies = out_ref.shape[0]
    for copy in range(copies):
        for tile in range(TILES):
            out_ref[copy, tile] = half_ref[:, tile * LANES : (tile + 1) * LANES]
        out_ref[copy, TILES] = packed


def project_kernel(
    last,
    core_ref,
    block_ref,
    state_ref,
    inverse_ref,
    gain_ref,
    value_ref,
    critic_ref,
    policy_ref,
    *rest,
):
    if last:
        sums_in, value_in, top_in, action_ref, *rest = rest
        logits_ref, totals_ref, own_ref, value_acc, normed_ref = rest
    else:
        logits_ref, value_acc, normed_ref = rest
    step = pl.program_id(0)
    tokens = normed_ref.shape[0]
    half = core_ref[0]
    inverse = inverse_column(half, inverse_ref)
    value_part = jnp.zeros((tokens, LANES), f32)
    for tile in range(CHUNK_TILES):
        where = slice(tile * LANES, (tile + 1) * LANES)
        normed = normed_tile(half, state_ref, tile, inverse, gain_ref)
        normed_ref[:, where] = normed
        value_part = value_part + normed.astype(f32) * value_ref[:, where].astype(f32)
    left = normed_ref[...]
    width = critic_ref.shape[1]
    critic = jnp.dot(left, critic_ref[...], preferred_element_type=f32)
    policy = jnp.dot(left, policy_ref[...], preferred_element_type=f32)

    @pl.when(step == 0)
    def _():
        value_acc[...] = value_part
        if last:
            logits_ref[:, :width] = sums_in[:, :width] + critic
            logits_ref[:, width:] = sums_in[:, width:] + policy
        else:
            logits_ref[:, :width] = critic
            logits_ref[:, width:] = policy

    @pl.when(step > 0)
    def _():
        value_acc[...] += value_part
        logits_ref[:, :width] += critic
        logits_ref[:, width:] += policy

    if last:

        @pl.when(step == CHUNKS - 1)
        def _():
            critic_logits = logits_ref[:, :width]
            policy_logits = logits_ref[:, width:]
            critic_top = jnp.max(critic_logits, axis=1, keepdims=True)
            policy_top = jnp.max(policy_logits, axis=1, keepdims=True)
            critic_total = jnp.sum(jnp.exp(critic_logits - critic_top), axis=1, keepdims=True)
            policy_total = jnp.sum(jnp.exp(policy_logits - policy_top), axis=1, keepdims=True)
            column = lax.broadcasted_iota(jnp.int32, (tokens, width), 1) + block_ref[0] * width
            action = to_columns(action_ref[...])[:, 0:1].astype(jnp.int32)
            taken = jnp.sum(
                jnp.where(column == action, critic_logits, 0.0), axis=1, keepdims=True
            )
            value = jnp.sum(value_in[...], axis=1, keepdims=True) + jnp.sum(
                value_acc[...], axis=1, keepdims=True
            )
            weight_top = jnp.broadcast_to(
                jnp.max(top_in[...], axis=1, keepdims=True), (tokens, 1)
            )
            packed = jnp.transpose(
                lane_pack(
                    [
                        critic_top,
                        policy_top,
                        critic_total,
                        policy_total,
                        taken,
                        weight_top,
                        value,
                    ]
                )
            )[:8]
            own_ref[...] = packed
            for copy in range(totals_ref.shape[0]):
                totals_ref[copy] = packed


def largest_kernel(critic_ref, policy_ref, top_ref):
    width = critic_ref.shape[1]
    largest = jnp.maximum(jnp.abs(critic_ref[...]), jnp.abs(policy_ref[...]))
    largest = jnp.max(largest.reshape(-1, 16, width), axis=0).astype(f32)
    largest = jnp.max(largest, axis=0, keepdims=True)
    step = pl.program_id(0)

    @pl.when(step == 0)
    def _():
        top_ref[...] = largest

    @pl.when(step > 0)
    def _():
        top_ref[...] = jnp.maximum(top_ref[...], largest)


def merge_parts(parts):
    tops = parts[:, 0:2]
    top = jnp.max(tops, axis=0)
    total = jnp.sum(parts[:, 2:4] * jnp.exp(tops - top[None]), axis=0)
    taken = jnp.sum(parts[:, 4:5], axis=0)
    weight_top = jnp.max(parts[:, 5:6], axis=0)
    return top, total, taken, weight_top


def merge_kernel(parts_ref, out_ref):
    tokens = parts_ref.shape[2]
    packed = jnp.concatenate([*merge_parts(parts_ref[...]), jnp.zeros((2, tokens), f32)], axis=0)
    for copy in range(out_ref.shape[0]):
        out_ref[copy] = packed


def turn(left, right):
    return lax.dot_general(left, right, (((1,), (1,)), ((), ())), preferred_element_type=f32)


def part_kernel(with_grads, core_ref, block_ref, *refs):
    if with_grads:
        parts_ref, own_ref, info_ref, logits_ref, *refs = refs
        state_ref, inverse_ref, critic_ref, policy_ref, out_ref, grads_ref, column_ref, gain_acc = refs
    else:
        grads_ref, column_ref, *refs = refs
        state_ref, inverse_ref, critic_ref, policy_ref, out_ref, gain_acc = refs
    step = pl.program_id(0)
    tokens = grads_ref.shape[0]
    width = critic_ref.shape[1]
    groups, _, rows, _ = out_ref.shape

    if with_grads:

        @pl.when(step == 0)
        def _():
            top, total, critic_taken, weight_top = merge_parts(parts_ref[...])
            values = own_ref[6:7]
            action, reward, done, live = (info_ref[k : k + 1] for k in range(4))
            place = lax.broadcasted_iota(jnp.int32, (1, tokens), 1)
            next_values = jnp.where(place == tokens - 1, 0.0, pltpu.roll(values, tokens - 1, 1))
            target = reward_step * reward + discount * (1.0 - done) * next_values
            advantage = critic_taken - values
            weights = jnp.where(advantage >= 0.0, expectile, 1.0 - expectile)
            value_coef = live * -2.0 * weights * advantage
            critic_coef = live * (2.0 * (critic_taken - target) - conservative)
            bound = (2.5 + jnp.abs(critic_coef)) * jnp.maximum(weight_top, 1e-20)
            gain_bound = jnp.sum(bound, axis=1, keepdims=True) * unit_limit
            first = to_columns(
                jnp.concatenate(
                    [
                        value_coef,
                        half_limit / bound,
                        bound / half_limit,
                        jnp.broadcast_to(half_limit / gain_bound, (1, tokens)),
                        jnp.broadcast_to(gain_bound / half_limit, (1, tokens)),
                        critic_coef,
                        action,
                        live,
                    ],
                    axis=0,
                )
            )
            column_ref[...] = first
            second = to_columns(
                jnp.concatenate([top, total, jnp.zeros((4, tokens), f32)], axis=0)
            )
            coef = first[:, 5:6]
            live_column = first[:, 7:8]
            column = lax.broadcasted_iota(jnp.int32, (tokens, width), 1) + block_ref[0] * width
            chosen = (column == first[:, 6:7].astype(jnp.int32)).astype(f32)
            critic_probs = jnp.exp(logits_ref[:, :width] - second[:, 0:1]) / second[:, 2:3]
            policy_probs = jnp.exp(logits_ref[:, width:] - second[:, 1:2]) / second[:, 3:4]
            grads_ref[:, :width] = (
                conservative * live_column * critic_probs + coef * chosen
            ).astype(bf16)
            grads_ref[:, width:] = (live_column * (policy_probs - chosen)).astype(bf16)

    @pl.when(step < CHUNKS)
    def _():
        half = core_ref[0]
        side = math.isqrt(groups)
        inverse = inverse_column(half, inverse_ref)
        part = turn(grads_ref[:, :width], critic_ref[...]) + turn(
            grads_ref[:, width:], policy_ref[...]
        )
        scale = column_ref[:, 1:2]
        gains = []
        for tile in range(CHUNK_TILES):
            block = part[:, tile * LANES : (tile + 1) * LANES]
            scaled = block * scale
            for group in range(groups):
                out_ref[reduced_place(half, group, side), tile] = scaled[
                    group * rows : (group + 1) * rows
                ]
            unit = gathered_tile(half, state_ref, tile) * inverse
            gains.append(jnp.sum(block * unit, axis=0, keepdims=True))
        gain_acc[pl.ds(pl.multiple_of(step * CHUNK_TILES, CHUNK_TILES), CHUNK_TILES)] = (
            jnp.concatenate(gains, axis=0)
        )

    @pl.when(step == CHUNKS)
    def _():
        gain = (gain_acc[...] * column_ref[0:1, 3:4]).reshape(TILES // rows, rows, LANES)
        for group in range(groups):
            out_ref[group, : TILES // rows] = gain


def weights_kernel(
    core_ref,
    mine_ref,
    mine_inverse_ref,
    other_ref,
    other_inverse_ref,
    gain_ref,
    grads_ref,
    column_ref,
    critic_ref,
    value_ref,
    extra_ref,
    normed_ref,
):
    step = pl.program_id(0)
    coef = column_ref[:, 0:1]

    def write(half, state_ref, inverse):
        for tile in range(CHUNK_TILES):
            where = slice(tile * LANES, (tile + 1) * LANES)
            normed = normed_tile(half, state_ref, tile, inverse, gain_ref)
            normed_ref[:, where] = normed
            value_ref[:, where] = jnp.sum(normed.astype(f32) * coef, axis=0, keepdims=True)
        critic_ref[...] = lax.dot_general(
            normed_ref[...], grads_ref[...], (((0,), (0,)), ((), ())), preferred_element_type=f32
        ).astype(bf16)

    @pl.when(step < CHUNKS)
    def _():
        half = core_ref[0]
        inverse = inverse_column(half, mine_inverse_ref)
        write(half, mine_ref, inverse)
        weighted = inverse * coef
        extra_ref[...] = jnp.concatenate(
            [
                jnp.sum(gathered_tile(half, mine_ref, tile) * weighted, axis=0, keepdims=True)
                for tile in range(CHUNK_TILES)
            ],
            axis=0,
        )

    @pl.when(step >= CHUNKS)
    def _():
        half = 1 - core_ref[0]
        write(half, other_ref, inverse_column(half, other_inverse_ref))


def split_kernel(block_ref, out_ref):
    peers = out_ref.shape[0]
    rows = 2 * peers
    for peer in range(peers):
        for k in range(2):
            out_ref[peer, k * TILES : (k + 1) * TILES] = block_ref[
                pl.ds(2 * peer + k, TILES, stride=rows)
            ]
        out_ref[peer, 2 * TILES :] = block_ref[TILES * rows :]


def finish_kernel(
    core_ref,
    column_ref,
    own_ref,
    far_ref,
    own_extra_ref,
    far_extra_ref,
    state_ref,
    weight_ref,
    value_ref,
    hidden_ref,
    gain_ref,
):
    first = core_ref[0] == 0
    own_half = jnp.where(first, own_ref[:TILES], own_ref[TILES : 2 * TILES])
    far_half = jnp.where(first, far_ref[:TILES], far_ref[TILES : 2 * TILES])
    row = jnp.concatenate(
        [jnp.where(first, own_half, far_half), jnp.where(first, far_half, own_half)], axis=0
    )
    value_coef = column_ref[:, 0:1]
    row_back = column_ref[:, 2:3]
    gain_back = column_ref[:, 4:5]
    value = value_ref[...].astype(f32)
    own_gain = own_ref[2 * TILES :] * gain_back
    far_gain = far_ref[2 * TILES :] * gain_back
    own_extra = own_extra_ref[...]
    far_extra = far_extra_ref[...]
    gain_ref[:TILES] = (
        jnp.where(first, own_gain, far_gain)
        + jnp.where(first, own_extra, far_extra) * value[:TILES]
    )
    gain_ref[TILES:] = (
        jnp.where(first, far_gain, own_gain)
        + jnp.where(first, far_extra, own_extra) * value[TILES:]
    )
    state = state_ref[...].astype(f32)
    mean = jnp.sum(jnp.sum(state * state, axis=1, keepdims=True), axis=0, keepdims=True) / D
    inverse = lax.rsqrt(mean + epsilon)
    unit = state * inverse
    normed_grad = row * row_back + value_coef * value
    scaled = normed_grad * weight_ref[...].astype(f32)
    row_dot = jnp.sum(jnp.sum(scaled * unit, axis=1, keepdims=True), axis=0, keepdims=True)
    grad = inverse * (scaled - unit * row_dot / D)
    for tile in range(2 * TILES):
        hidden_ref[:, tile * LANES : (tile + 1) * LANES] = grad[tile : tile + 1].astype(bf16)


def contract_tokens(left_side, right_side):
    return lax.dot_general(
        left_side, right_side, (((0,), (0,)), ((), ())), preferred_element_type=f32
    )


def body(
    hidden_state,
    norm_gain,
    critic_weight,
    policy_weight,
    value_weight,
    actions,
    rewards,
    done_flags,
    pad_mask,
):
    dp_size = lax.axis_size("dp")
    mp_size = lax.axis_size("mp")
    chip_count = mp_size // 2
    dp_index = lax.axis_index("dp")
    mp_index = lax.axis_index("mp")
    core = mp_index % 2
    core_swap = [(i, i ^ 1) for i in range(mp_size)]
    chip_groups = [[c + 2 * k for k in range(chip_count)] for c in range(2)]
    rows = hidden_state.shape[0]
    tokens = rows * dp_size
    width = critic_weight.shape[1]
    block_index = dp_index * mp_size + mp_index
    core_scalar = core.astype(jnp.int32).reshape(1)
    far_scalar = 1 - core_scalar
    block_scalar = block_index.astype(jnp.int32).reshape(1)

    def swap(array):
        return lax.ppermute(array, "mp", core_swap)

    gain_row = norm_gain.reshape(1, D)
    value_row = value_weight.reshape(1, D)
    info = jnp.stack([actions, rewards, done_flags, pad_mask] + [pad_mask] * 4).astype(f32)

    side = math.isqrt(dp_size)

    def axis_groups(turned):
        groups = []
        for c in range(2):
            for z in range(chip_count):
                for line in range(side):
                    along_x = (c == 0) != turned
                    groups.append(
                        [
                            (k * side + line if along_x else line * side + k) * mp_size + 2 * z + c
                            for k in range(side)
                        ]
                    )
        return groups

    def exchange(array, turned):
        flat = array.reshape(side, -1, LANES)
        return lax.all_to_all(
            flat, ("dp", "mp"), 0, 0, axis_index_groups=axis_groups(turned)
        ).reshape(array.shape)

    with jax.named_scope("norm"):
        copies = pl.pallas_call(
            norm_kernel,
            out_shape=jax.ShapeDtypeStruct((side, TILES + 1, rows, LANES), bf16),
            grid_spec=pltpu.PrefetchScalarGridSpec(
                num_scalar_prefetch=1,
                grid=(1,),
                in_specs=[
                    pl.BlockSpec((rows, D), lambda i, core: (0, 0)),
                    pl.BlockSpec((rows, HALF), lambda i, core: (0, core[0])),
                ],
                out_specs=whole((side, TILES + 1, rows, LANES)),
            ),
            compiler_params=roomy,
        )(core_scalar, hidden_state, hidden_state)

    with jax.named_scope("gather"):
        line = exchange(copies, False)
        line, critic_weight, policy_weight = lax.optimization_barrier(
            (line, critic_weight, policy_weight)
        )
        mine = exchange(jnp.broadcast_to(line[None], (side,) + line.shape), True).reshape(
            dp_size, TILES + 1, rows, LANES
        )
        weight_spec = pl.BlockSpec((CHUNK, width), lambda i: (i, 0))
        largest = pl.pallas_call(
            largest_kernel,
            out_shape=jax.ShapeDtypeStruct((1, width), f32),
            grid=(D // CHUNK,),
            in_specs=[weight_spec] * 2,
            out_specs=whole((1, width)),
            compiler_params=roomy,
            cost_estimate=pl.CostEstimate(
                flops=2**34, bytes_accessed=4 * D * width, transcendentals=0
            ),
        )(critic_weight, policy_weight)
        mine, largest = lax.optimization_barrier((mine, largest))
        other = swap(mine)

    state_block = (dp_size, CHUNK_TILES, rows, LANES)
    inverse_spec = pl.BlockSpec((dp_size, 1, rows, LANES), lambda i, *_: (0, TILES, 0, 0))

    def project(which, states, extra):
        last = bool(extra)
        weight_spec = pl.BlockSpec((CHUNK, width), lambda i, half, _: (half[0] * CHUNKS + i, 0))
        feature_spec = pl.BlockSpec((1, CHUNK), lambda i, half, _: (0, half[0] * CHUNKS + i))
        logits_shape = (tokens, 2 * width)
        out_shape = [jax.ShapeDtypeStruct(logits_shape, f32)]
        out_specs = [whole(logits_shape)]
        scratch = [pltpu.VMEM((tokens, CHUNK), bf16)]
        if last:
            out_shape += [
                jax.ShapeDtypeStruct((mp_size, 8, tokens), f32),
                jax.ShapeDtypeStruct((8, tokens), f32),
            ]
            out_specs += [whole((mp_size, 8, tokens)), whole((8, tokens))]
            scratch = [pltpu.VMEM((tokens, LANES), f32)] + scratch
        else:
            out_shape += [jax.ShapeDtypeStruct((tokens, LANES), f32)]
            out_specs += [whole((tokens, LANES))]
        return pl.pallas_call(
            functools.partial(project_kernel, last),
            out_shape=out_shape,
            grid_spec=pltpu.PrefetchScalarGridSpec(
                num_scalar_prefetch=2,
                grid=(CHUNKS,),
                in_specs=[
                    pl.BlockSpec(state_block, lambda i, *_: (0, i, 0, 0)),
                    inverse_spec,
                    feature_spec,
                    feature_spec,
                    weight_spec,
                    weight_spec,
                ]
                + [whole(array.shape) for array in extra],
                out_specs=out_specs,
                scratch_shapes=scratch,
            ),
            compiler_params=roomy,
            cost_estimate=pl.CostEstimate(
                flops=2 * tokens * HALF * 2 * width,
                bytes_accessed=2 * (2 * HALF * width + 2 * tokens * HALF),
                transcendentals=0,
            ),
        )(
            which,
            block_scalar,
            states,
            states,
            gain_row,
            value_row,
            critic_weight,
            policy_weight,
            *extra,
        )

    with jax.named_scope("logits"):
        sums, value_lanes = project(core_scalar, mine, [])
        logits, totals, own_rows = project(
            far_scalar, other, [sums, value_lanes, largest, info]
        )

    with jax.named_scope("totals"):
        totals = lax.all_to_all(totals, "mp", 0, 0)
        totals = pl.pallas_call(
            merge_kernel,
            out_shape=jax.ShapeDtypeStruct((dp_size, 8, tokens), f32),
            compiler_params=roomy,
        )(totals)
        totals = lax.all_to_all(totals, "dp", 0, 0)

    matmul_cost = pl.CostEstimate(
        flops=2 * tokens * HALF * 2 * width,
        bytes_accessed=2 * (2 * HALF * width + 2 * tokens * HALF),
        transcendentals=0,
    )
    part_shape = (dp_size, TILES + TILES // rows, rows, LANES)

    def part(which, states, extra, with_grads):
        def chunk(i):
            return jnp.minimum(i, CHUNKS - 1)

        weight_spec = pl.BlockSpec(
            (CHUNK, width), lambda i, half, _: (half[0] * CHUNKS + chunk(i), 0)
        )
        out_shape = [jax.ShapeDtypeStruct(part_shape, f32)]
        out_specs = [pl.BlockSpec(state_block, lambda i, *_: (0, i, 0, 0))]
        if with_grads:
            out_shape += [
                jax.ShapeDtypeStruct((tokens, 2 * width), bf16),
                jax.ShapeDtypeStruct((tokens, LANES), f32),
            ]
            out_specs += [whole((tokens, 2 * width)), whole((tokens, LANES))]
        return pl.pallas_call(
            functools.partial(part_kernel, with_grads),
            out_shape=out_shape,
            grid_spec=pltpu.PrefetchScalarGridSpec(
                num_scalar_prefetch=2,
                grid=(CHUNKS + 1,),
                in_specs=[whole(array.shape) for array in extra]
                + [
                    pl.BlockSpec(state_block, lambda i, *_: (0, chunk(i), 0, 0)),
                    inverse_spec,
                    weight_spec,
                    weight_spec,
                ],
                out_specs=out_specs,
                scratch_shapes=[pltpu.VMEM((TILES, LANES), f32)],
            ),
            compiler_params=roomy,
            cost_estimate=matmul_cost,
        )(which, block_scalar, *extra, states, states, critic_weight, policy_weight)

    with jax.named_scope("reduce"):
        part_other, grads, column = part(
            far_scalar, other, [totals, own_rows, info, logits], True
        )
        arrived = swap(part_other.astype(f16))
        (part_mine,) = part(core_scalar, mine, [grads, column], False)
        joined = (part_mine + arrived.astype(f32)).astype(f16)
        lines = exchange(joined.reshape((side, side) + part_shape[1:]), False)

    with jax.named_scope("weights"):

        def own_chunk(i):
            return jnp.minimum(i, CHUNKS - 1)

        def far_chunk(i):
            return jnp.maximum(i - CHUNKS, 0)

        def out_chunk(i, half):
            return jnp.where(
                i < CHUNKS, half[0] * CHUNKS + i, (1 - half[0]) * CHUNKS + i - CHUNKS
            )

        grad_critic, grad_value, extra = pl.pallas_call(
            weights_kernel,
            out_shape=[
                jax.ShapeDtypeStruct((D, width), bf16),
                jax.ShapeDtypeStruct((1, D), f32),
                jax.ShapeDtypeStruct((TILES, LANES), f32),
            ],
            grid_spec=pltpu.PrefetchScalarGridSpec(
                num_scalar_prefetch=1,
                grid=(2 * CHUNKS,),
                in_specs=[
                    pl.BlockSpec(state_block, lambda i, half: (0, own_chunk(i), 0, 0)),
                    inverse_spec,
                    pl.BlockSpec(state_block, lambda i, half: (0, far_chunk(i), 0, 0)),
                    inverse_spec,
                    pl.BlockSpec((1, CHUNK), lambda i, half: (0, out_chunk(i, half))),
                    pl.BlockSpec((tokens, width), lambda i, half: (0, 0)),
                    whole((tokens, LANES)),
                ],
                out_specs=[
                    pl.BlockSpec((CHUNK, width), lambda i, half: (out_chunk(i, half), 0)),
                    pl.BlockSpec((1, CHUNK), lambda i, half: (0, out_chunk(i, half))),
                    pl.BlockSpec((CHUNK_TILES, LANES), lambda i, half: (own_chunk(i), 0)),
                ],
                scratch_shapes=[pltpu.VMEM((tokens, CHUNK), bf16)],
            ),
            compiler_params=roomy,
            cost_estimate=pl.CostEstimate(
                flops=2 * tokens * D * width,
                bytes_accessed=2 * (D * width + 2 * tokens * D),
                transcendentals=0,
            ),
        )(core_scalar, mine, mine, other, other, gain_row, grads, column)
        far_extra = swap(extra)
        token = lax.dynamic_slice(column, (block_index, 0), (1, LANES))
        state_row = lax.dynamic_slice_in_dim(hidden_state, mp_index, 1, 0).reshape(
            2 * TILES, LANES
        )
        lines, grad_critic, grad_value, far_extra, token, state_row = lax.optimization_barrier(
            (lines, grad_critic, grad_value, far_extra, token, state_row)
        )

    with jax.named_scope("lines"):
        blocks = exchange(jnp.sum(lines.astype(f32), axis=0).astype(f16), True)

    with jax.named_scope("chips"):
        block = jnp.sum(blocks.astype(f32), axis=0).reshape(-1, LANES)
        shares = pl.pallas_call(
            split_kernel,
            out_shape=jax.ShapeDtypeStruct((chip_count, 3 * TILES, LANES), f32),
            compiler_params=roomy,
        )(block)
        shares = lax.all_to_all(
            shares.astype(f16), "mp", 0, 0, axis_index_groups=chip_groups
        )
        own = jnp.sum(shares.astype(f32), axis=0)
        far = swap(own)

    with jax.named_scope("finish"):
        smem = pl.BlockSpec(memory_space=pltpu.SMEM)
        vmem = pl.BlockSpec(memory_space=pltpu.VMEM)
        grad_hidden, grad_gain = pl.pallas_call(
            finish_kernel,
            out_shape=[
                jax.ShapeDtypeStruct((1, D), bf16),
                jax.ShapeDtypeStruct((2 * TILES, LANES), f32),
            ],
            in_specs=[smem] + [vmem] * 8,
            compiler_params=roomy,
        )(
            core_scalar,
            token,
            own,
            far,
            extra,
            far_extra,
            state_row,
            norm_gain.reshape(2 * TILES, LANES),
            value_weight.reshape(2 * TILES, LANES),
        )
    return (grad_hidden, grad_gain.reshape(D), grad_critic, grad_value.reshape(D))


def solution(mesh):
    placed = (
        P("dp", None),
        P(),
        P(None, ("dp", "mp")),
        P(None, ("dp", "mp")),
        P(),
        P(),
        P(),
        P(),
        P(),
    )
    return jax.shard_map(
        body,
        mesh=mesh,
        in_specs=placed,
        out_specs=(P(("dp", "mp"), None), P(), P(None, ("dp", "mp")), P()),
        check_vma=False,
    )
```

```python
import functools
import math

import jax
import jax.numpy as jnp
from jax import lax
from jax.experimental import pallas as pl
from jax.experimental.pallas import tpu as pltpu
from jax.sharding import PartitionSpec as P

D = 8192
HALF = D // 2
LANES = 128
TILES = HALF // LANES
CHUNK_TILES = 8
CHUNK = CHUNK_TILES * LANES
CHUNKS = TILES // CHUNK_TILES


discount = 0.99
expectile = 0.7
conservative = 0.5
reward_step = 0.5
epsilon = 1e-05
unit_limit = 91.0
half_limit = 32768.0

f32 = jnp.float32
bf16 = jnp.bfloat16
f16 = jnp.float16

roomy = pltpu.CompilerParams(vmem_limit_bytes=14 * 1024 * 1024)


def whole(shape):
    return pl.BlockSpec(shape, lambda *_: (0,) * len(shape))


def to_columns(rows):
    tokens = rows.shape[1]
    filled = jnp.concatenate([rows, jnp.zeros((LANES - rows.shape[0], tokens), f32)], axis=0)
    return jnp.transpose(filled)


def lane_pack(columns):
    tokens = columns[0].shape[0]
    lane = lax.broadcasted_iota(jnp.int32, (tokens, LANES), 1)
    packed = jnp.zeros((tokens, LANES), f32)
    for k, column in enumerate(columns):
        packed = jnp.where(lane == k, column, packed)
    return packed


def half_of(where_ref):
    return lax.rem(where_ref[0], 2)


def gathered_place(where_ref, group, side):
    own = lax.div(where_ref[0], 2)
    x, y = divmod(group, side)
    return jnp.where(
        half_of(where_ref) == 0,
        y * side + lax.rem(x - lax.div(own, side) + side, side),
        x * side + lax.rem(y - lax.rem(own, side) + side, side),
    )


def reduced_place(half, group, side):
    x, y = divmod(group, side)
    return jnp.where(half == 0, x * side + y, y * side + x)


def group_rows(group, rows):
    return slice(group * rows, (group + 1) * rows)


def spread_inverse(where_ref, inverse_ref, out_ref):
    groups, _, rows, _ = inverse_ref.shape
    side = math.isqrt(groups)
    for group in range(groups):
        parts = inverse_ref[gathered_place(where_ref, group, side), 0].astype(f32)
        inverse = parts[:, 0:1] + parts[:, 1:2] + parts[:, 2:3]
        out_ref[group_rows(group, rows)] = jnp.broadcast_to(inverse, (rows, LANES))


def norm_kernel(core_ref, state_ref, half_ref, out_ref):
    state = state_ref[...].astype(f32)
    mean = jnp.sum(state * state, axis=1, keepdims=True) / D
    inverse = lax.rsqrt(mean + epsilon)
    high = inverse.astype(bf16).astype(f32)
    middle = (inverse - high).astype(bf16).astype(f32)
    low = inverse - high - middle
    packed = lane_pack([high, middle, low]).astype(bf16)
    for tile in range(TILES):
        out_ref[tile] = half_ref[:, tile * LANES : (tile + 1) * LANES]
    out_ref[TILES] = packed


def column_tops(weight):
    width = weight.shape[1]
    largest = jnp.max(jnp.abs(weight).reshape(-1, 16, width), axis=0).astype(f32)
    return jnp.max(largest, axis=0, keepdims=True)


def gather_sum(step, ref, part):
    @pl.when(step == 0)
    def _():
        ref[...] = part

    @pl.when(step > 0)
    def _():
        ref[...] += part


def gather_top(step, ref, part):
    @pl.when(step == 0)
    def _():
        ref[...] = part

    @pl.when(step > 0)
    def _():
        ref[...] = jnp.maximum(ref[...], part)


def normed_chunk(core_ref, state_ref, inverse_ref, gain_ref, value_ref, normed_ref, spread, acc):
    step = pl.program_id(0)
    half = half_of(core_ref)
    groups, _, rows, _ = state_ref.shape
    side = math.isqrt(groups)

    @pl.when(step == 0)
    def _():
        spread_inverse(core_ref, inverse_ref, spread)
        acc[...] = jnp.zeros_like(acc)

    gains, values = [], []
    for tile in range(CHUNK_TILES):
        where = slice(tile * LANES, (tile + 1) * LANES)
        gains.append(gain_ref[:, where].astype(f32))
        values.append(value_ref[:, where].astype(f32))
    for group in range(groups):
        place = gathered_place(core_ref, group, side)
        lines = group_rows(group, rows)
        inverse = spread[lines]
        part = acc[lines]
        for tile in range(CHUNK_TILES):
            unit = state_ref[place, tile].astype(f32) * inverse
            normed = (unit * gains[tile]).astype(bf16)
            normed_ref[lines, tile * LANES : (tile + 1) * LANES] = normed
            part = part + normed.astype(f32) * values[tile]
        acc[lines] = part


def normed_kernel(
    core_ref, state_ref, inverse_ref, gain_ref, value_ref, normed_ref, value_acc, spread
):
    normed_chunk(
        core_ref, state_ref, inverse_ref, gain_ref, value_ref, normed_ref, spread, value_acc
    )


def head_kernel(core_ref, normed_ref, weight_ref, sums_ref, top_ref):
    step = pl.program_id(0)
    part = jnp.dot(normed_ref[...], weight_ref[...], preferred_element_type=f32)
    gather_sum(step, sums_ref, part)
    gather_top(step, top_ref, column_tops(weight_ref[...]))


def totals_kernel(
    core_ref,
    block_ref,
    state_ref,
    inverse_ref,
    gain_ref,
    value_ref,
    critic_ref,
    policy_ref,
    critic_in,
    policy_in,
    value_in,
    critic_top_in,
    policy_top_in,
    info_ref,
    powers_ref,
    totals_ref,
    own_ref,
    value_acc,
    top_ref,
    normed_ref,
    spread,
):
    step = pl.program_id(0)
    tokens = normed_ref.shape[0]
    width = critic_ref.shape[1]
    normed_chunk(
        core_ref, state_ref, inverse_ref, gain_ref, value_ref, normed_ref, spread, value_acc
    )
    critic = jnp.dot(normed_ref[...], critic_ref[...], preferred_element_type=f32)
    policy = jnp.dot(normed_ref[...], policy_ref[...], preferred_element_type=f32)
    gather_top(
        step, top_ref, jnp.maximum(column_tops(critic_ref[...]), column_tops(policy_ref[...]))
    )

    @pl.when(step == 0)
    def _():
        powers_ref[:, :width] = critic_in[...] + critic
        powers_ref[:, width:] = policy_in[...] + policy

    @pl.when(step > 0)
    def _():
        powers_ref[:, :width] += critic
        powers_ref[:, width:] += policy

    @pl.when(step == CHUNKS - 1)
    def _():
        critic_logits = powers_ref[:, :width]
        policy_logits = powers_ref[:, width:]
        critic_top = jnp.max(critic_logits, axis=1, keepdims=True)
        policy_top = jnp.max(policy_logits, axis=1, keepdims=True)
        column = lax.broadcasted_iota(jnp.int32, (tokens, width), 1) + block_ref[0] * width
        action = to_columns(info_ref[...])[:, 0:1].astype(jnp.int32)
        taken = jnp.sum(jnp.where(column == action, critic_logits, 0.0), axis=1, keepdims=True)
        critic_powers = jnp.exp(critic_logits - critic_top)
        policy_powers = jnp.exp(policy_logits - policy_top)
        powers_ref[:, :width] = critic_powers
        powers_ref[:, width:] = policy_powers
        value = jnp.sum(value_in[...], axis=1, keepdims=True) + jnp.sum(
            value_acc[...], axis=1, keepdims=True
        )
        top = jnp.maximum(top_ref[...], jnp.maximum(critic_top_in[...], policy_top_in[...]))
        weight_top = jnp.broadcast_to(jnp.max(top, axis=1, keepdims=True), (tokens, 1))
        packed = jnp.transpose(
            lane_pack(
                [
                    critic_top,
                    policy_top,
                    jnp.sum(critic_powers, axis=1, keepdims=True),
                    jnp.sum(policy_powers, axis=1, keepdims=True),
                    taken,
                    weight_top,
                    value,
                ]
            )
        )[:8]
        own_ref[...] = packed
        for copy in range(totals_ref.shape[0]):
            totals_ref[copy] = packed


def merge_parts(parts):
    tops = parts[:, 0:2]
    top = jnp.max(tops, axis=0)
    total = jnp.sum(parts[:, 2:4] * jnp.exp(tops - top[None]), axis=0)
    taken = jnp.sum(parts[:, 4:5], axis=0)
    weight_top = jnp.max(parts[:, 5:6], axis=0)
    return top, total, taken, weight_top


def merge_kernel(parts_ref, out_ref):
    tokens = parts_ref.shape[2]
    packed = jnp.concatenate([*merge_parts(parts_ref[...]), jnp.zeros((2, tokens), f32)], axis=0)
    for copy in range(out_ref.shape[0]):
        out_ref[copy] = packed


def turn(left, right):
    return lax.dot_general(left, right, (((1,), (1,)), ((), ())), preferred_element_type=f32)


def part_kernel(with_grads, core_ref, block_ref, *refs):
    if with_grads:
        parts_ref, own_ref, info_ref, powers_ref, *refs = refs
        state_ref, inverse_ref, critic_ref, policy_ref, out_ref, grads_ref, column_ref, *refs = refs
    else:
        grads_ref, column_ref, *refs = refs
        state_ref, inverse_ref, critic_ref, policy_ref, out_ref, *refs = refs
    gain_acc, spread, scales = refs
    step = pl.program_id(0)
    tokens = grads_ref.shape[0]
    width = critic_ref.shape[1]
    groups, _, rows, _ = out_ref.shape

    if with_grads:

        @pl.when(step == 0)
        def _():
            top, total, critic_taken, weight_top = merge_parts(parts_ref[...])
            values = own_ref[6:7]
            action, reward, done, live = (info_ref[k : k + 1] for k in range(4))
            place = lax.broadcasted_iota(jnp.int32, (1, tokens), 1)
            next_values = jnp.where(place == tokens - 1, 0.0, pltpu.roll(values, tokens - 1, 1))
            target = reward_step * reward + discount * (1.0 - done) * next_values
            advantage = critic_taken - values
            weights = jnp.where(advantage >= 0.0, expectile, 1.0 - expectile)
            value_coef = live * -2.0 * weights * advantage
            critic_coef = live * (2.0 * (critic_taken - target) - conservative)
            bound = (2.5 + jnp.abs(critic_coef)) * jnp.maximum(weight_top, 1e-20)
            gain_bound = jnp.sum(bound, axis=1, keepdims=True) * unit_limit
            first = to_columns(
                jnp.concatenate(
                    [
                        value_coef,
                        half_limit / bound,
                        bound / half_limit,
                        jnp.broadcast_to(half_limit / gain_bound, (1, tokens)),
                        jnp.broadcast_to(gain_bound / half_limit, (1, tokens)),
                        critic_coef,
                        action,
                        live,
                    ],
                    axis=0,
                )
            )
            column_ref[...] = first
            second = to_columns(
                jnp.concatenate(
                    [jnp.exp(own_ref[0:2] - top) / total, jnp.zeros((6, tokens), f32)], axis=0
                )
            )
            coef = first[:, 5:6]
            live_column = first[:, 7:8]
            column = lax.broadcasted_iota(jnp.int32, (tokens, width), 1) + block_ref[0] * width
            chosen = (column == first[:, 6:7].astype(jnp.int32)).astype(f32)
            critic_probs = powers_ref[:, :width] * second[:, 0:1]
            policy_probs = powers_ref[:, width:] * second[:, 1:2]
            grads_ref[:, :width] = (
                conservative * live_column * critic_probs + coef * chosen
            ).astype(bf16)
            grads_ref[:, width:] = (live_column * (policy_probs - chosen)).astype(bf16)

    half = half_of(core_ref)
    side = math.isqrt(groups)

    @pl.when(step == 0)
    def _():
        spread_inverse(core_ref, inverse_ref, spread)
        scales[...] = jnp.broadcast_to(column_ref[:, 1:2], scales.shape)

    @pl.when(step < CHUNKS)
    def _():
        part = turn(grads_ref[:, :width], critic_ref[...]) + turn(
            grads_ref[:, width:], policy_ref[...]
        )
        scale = scales[...]
        inverse = spread[...]
        gains = []
        for tile in range(CHUNK_TILES):
            block = part[:, tile * LANES : (tile + 1) * LANES]
            scaled = block * scale
            for group in range(groups):
                out_ref[reduced_place(half, group, side), tile] = scaled[group_rows(group, rows)]
            state = jnp.concatenate(
                [
                    state_ref[gathered_place(core_ref, group, side), tile].astype(f32)
                    for group in range(groups)
                ],
                axis=0,
            )
            gains.append(jnp.sum(block * (state * inverse), axis=0, keepdims=True))
        gain_acc[pl.ds(pl.multiple_of(step * CHUNK_TILES, CHUNK_TILES), CHUNK_TILES)] = (
            jnp.concatenate(gains, axis=0)
        )

    @pl.when(step == CHUNKS)
    def _():
        gain = (gain_acc[...] * column_ref[0:1, 3:4]).reshape(TILES // rows, rows, LANES)
        for group in range(groups):
            out_ref[group, : TILES // rows] = gain


def weights_kernel(far, core_ref, state_ref, inverse_ref, gain_ref, grads_ref, column_ref, *refs):
    if far:
        _, _, critic_ref, value_ref, normed_ref, spread, coefs = refs
    else:
        critic_ref, value_ref, extra_ref, normed_ref, spread, coefs = refs
    step = pl.program_id(0)
    half = half_of(core_ref)
    groups, _, rows, _ = state_ref.shape
    side = math.isqrt(groups)

    @pl.when(step == 0)
    def _():
        spread_inverse(core_ref, inverse_ref, spread)
        coefs[...] = jnp.broadcast_to(column_ref[:, 0:1], coefs.shape)

    extras = []
    for tile in range(CHUNK_TILES):
        where = slice(tile * LANES, (tile + 1) * LANES)
        gain = gain_ref[:, where].astype(f32)
        value = jnp.zeros((rows, LANES), f32)
        extra = jnp.zeros((rows, LANES), f32)
        for group in range(groups):
            lines = group_rows(group, rows)
            state = state_ref[gathered_place(core_ref, group, side), tile].astype(f32)
            unit = state * spread[lines]
            normed = (unit * gain).astype(bf16)
            normed_ref[lines, where] = normed
            coef = coefs[lines]
            value = value + normed.astype(f32) * coef
            extra = extra + unit * coef
        value_ref[:, where] = jnp.sum(value, axis=0, keepdims=True)
        extras.append(jnp.sum(extra, axis=0, keepdims=True))
    critic_ref[...] = lax.dot_general(
        normed_ref[...], grads_ref[...], (((0,), (0,)), ((), ())), preferred_element_type=f32
    ).astype(bf16)
    if not far:
        extra_ref[...] = jnp.concatenate(extras, axis=0)


def split_kernel(block_ref, out_ref):
    peers = out_ref.shape[0]
    rows = 2 * peers
    for peer in range(peers):
        for k in range(2):
            out_ref[peer, k * TILES : (k + 1) * TILES] = block_ref[
                pl.ds(2 * peer + k, TILES, stride=rows)
            ]
        out_ref[peer, 2 * TILES :] = block_ref[TILES * rows :]


def finish_kernel(
    core_ref,
    column_ref,
    own_ref,
    far_ref,
    own_extra_ref,
    far_extra_ref,
    state_ref,
    weight_ref,
    value_ref,
    hidden_ref,
    gain_ref,
):
    first = half_of(core_ref) == 0
    own_half = jnp.where(first, own_ref[:TILES], own_ref[TILES : 2 * TILES])
    far_half = jnp.where(first, far_ref[:TILES], far_ref[TILES : 2 * TILES])
    row = jnp.concatenate(
        [jnp.where(first, own_half, far_half), jnp.where(first, far_half, own_half)], axis=0
    )
    value_coef = column_ref[:, 0:1]
    row_back = column_ref[:, 2:3]
    gain_back = column_ref[:, 4:5]
    value = value_ref[...].astype(f32)
    own_gain = own_ref[2 * TILES :] * gain_back
    far_gain = far_ref[2 * TILES :] * gain_back
    own_extra = own_extra_ref[...]
    far_extra = far_extra_ref[...]
    gain_ref[:TILES] = (
        jnp.where(first, own_gain, far_gain)
        + jnp.where(first, own_extra, far_extra) * value[:TILES]
    )
    gain_ref[TILES:] = (
        jnp.where(first, far_gain, own_gain)
        + jnp.where(first, far_extra, own_extra) * value[TILES:]
    )
    state = state_ref[...].astype(f32)
    mean = jnp.sum(jnp.sum(state * state, axis=1, keepdims=True), axis=0, keepdims=True) / D
    inverse = lax.rsqrt(mean + epsilon)
    unit = state * inverse
    normed_grad = row * row_back + value_coef * value
    scaled = normed_grad * weight_ref[...].astype(f32)
    row_dot = jnp.sum(jnp.sum(scaled * unit, axis=1, keepdims=True), axis=0, keepdims=True)
    grad = inverse * (scaled - unit * row_dot / D)
    for tile in range(2 * TILES):
        hidden_ref[:, tile * LANES : (tile + 1) * LANES] = grad[tile : tile + 1].astype(bf16)


def contract_tokens(left_side, right_side):
    return lax.dot_general(
        left_side, right_side, (((0,), (0,)), ((), ())), preferred_element_type=f32
    )


def body(
    hidden_state,
    norm_gain,
    critic_weight,
    policy_weight,
    value_weight,
    actions,
    rewards,
    done_flags,
    pad_mask,
):
    dp_size = lax.axis_size("dp")
    mp_size = lax.axis_size("mp")
    chip_count = mp_size // 2
    dp_index = lax.axis_index("dp")
    mp_index = lax.axis_index("mp")
    core = mp_index % 2
    core_swap = [(i, i ^ 1) for i in range(mp_size)]
    chip_groups = [[c + 2 * k for k in range(chip_count)] for c in range(2)]
    rows = hidden_state.shape[0]
    tokens = rows * dp_size
    width = critic_weight.shape[1]
    block_index = dp_index * mp_size + mp_index
    side = math.isqrt(dp_size)
    def scalars(half):
        return (half + 2 * dp_index).astype(jnp.int32).reshape(1)

    core_scalar = scalars(core)
    far_scalar = scalars(1 - core)
    block_scalar = block_index.astype(jnp.int32).reshape(1)

    def swap(array):
        return lax.ppermute(array, "mp", core_swap)

    gain_row = norm_gain.reshape(1, D)
    value_row = value_weight.reshape(1, D)
    info = jnp.stack([actions, rewards, done_flags, pad_mask] + [pad_mask] * 4).astype(f32)

    def axis_groups(turned):
        groups = []
        for c in range(2):
            for z in range(chip_count):
                for line in range(side):
                    along_x = (c == 0) != turned
                    groups.append(
                        [
                            (k * side + line if along_x else line * side + k) * mp_size + 2 * z + c
                            for k in range(side)
                        ]
                    )
        return groups

    def shift(array, step):
        moves = []
        for dp in range(dp_size):
            x, y = divmod(dp, side)
            for mp in range(mp_size):
                if mp % 2 == 0:
                    target = (x + step) % side * side + y
                else:
                    target = x * side + (y + step) % side
                moves.append((dp * mp_size + mp, target * mp_size + mp))
        return lax.ppermute(array, ("dp", "mp"), moves)

    def exchange(array, turned):
        flat = array.reshape(side, -1, LANES)
        return lax.all_to_all(
            flat, ("dp", "mp"), 0, 0, axis_index_groups=axis_groups(turned)
        ).reshape(array.shape)

    def pack(array, is_row):
        squared = array * jnp.abs(array) * (1.0 / half_limit)
        return jnp.where(is_row, squared, array).astype(f16)

    def unpack(array, is_row):
        array = array.astype(f32)
        root = jnp.sqrt(jnp.abs(array) * half_limit)
        return jnp.where(is_row, jnp.where(array < 0.0, -root, root), array)

    tile_is_row = jnp.arange(TILES + TILES // rows)[:, None, None] < TILES
    share_is_row = jnp.arange(3 * TILES)[:, None] < 2 * TILES
    tile_is_row = jnp.broadcast_to(tile_is_row, (TILES + TILES // rows, rows, LANES))
    share_is_row = jnp.broadcast_to(share_is_row, (3 * TILES, LANES))

    with jax.named_scope("norm"):
        payload = pl.pallas_call(
            norm_kernel,
            out_shape=jax.ShapeDtypeStruct((TILES + 1, rows, LANES), bf16),
            grid_spec=pltpu.PrefetchScalarGridSpec(
                num_scalar_prefetch=1,
                grid=(1,),
                in_specs=[
                    pl.BlockSpec((rows, D), lambda i, core: (0, 0)),
                    pl.BlockSpec((rows, HALF), lambda i, core: (0, half_of(core))),
                ],
                out_specs=whole((TILES + 1, rows, LANES)),
            ),
            compiler_params=roomy,
        )(core_scalar, hidden_state, hidden_state)

    with jax.named_scope("gather"):
        line = jnp.stack([payload] + [shift(payload, -step) for step in range(1, side)])
        mine = exchange(jnp.broadcast_to(line[None], (side,) + line.shape), True).reshape(
            dp_size, TILES + 1, rows, LANES
        )
        other = swap(mine)

    state_block = (dp_size, CHUNK_TILES, rows, LANES)
    inverse_spec = pl.BlockSpec((dp_size, 1, rows, LANES), lambda i, *_: (0, TILES, 0, 0))

    logits_cost = pl.CostEstimate(
        flops=2 * tokens * HALF * width,
        bytes_accessed=2 * HALF * (width + tokens),
        transcendentals=0,
    )
    feature_spec = pl.BlockSpec((1, CHUNK), lambda i, half, *_: (0, half_of(half) * CHUNKS + i))
    weight_spec = pl.BlockSpec((CHUNK, width), lambda i, half, *_: (half_of(half) * CHUNKS + i, 0))
    normed_spec = pl.BlockSpec((tokens, CHUNK), lambda i, *_: (0, i))
    state_specs = [
        pl.BlockSpec(state_block, lambda i, *_: (0, i, 0, 0)),
        inverse_spec,
        feature_spec,
        feature_spec,
    ]
    sums_shape = jax.ShapeDtypeStruct((tokens, width), f32)
    top_shape = jax.ShapeDtypeStruct((1, width), f32)
    value_shape = jax.ShapeDtypeStruct((tokens, LANES), f32)

    with jax.named_scope("logits"):
        normed, value_lanes = pl.pallas_call(
            normed_kernel,
            out_shape=[jax.ShapeDtypeStruct((tokens, HALF), bf16), value_shape],
            grid_spec=pltpu.PrefetchScalarGridSpec(
                num_scalar_prefetch=1,
                grid=(CHUNKS,),
                in_specs=state_specs,
                out_specs=[normed_spec, whole(value_shape.shape)],
                scratch_shapes=[pltpu.VMEM((tokens, LANES), f32)],
            ),
            compiler_params=roomy,
            cost_estimate=pl.CostEstimate(
                flops=8 * tokens * HALF, bytes_accessed=4 * tokens * HALF, transcendentals=0
            ),
        )(core_scalar, mine, mine, gain_row, value_row)

        def head(weight):
            return pl.pallas_call(
                head_kernel,
                out_shape=[sums_shape, top_shape],
                grid_spec=pltpu.PrefetchScalarGridSpec(
                    num_scalar_prefetch=1,
                    grid=(CHUNKS,),
                    in_specs=[normed_spec, weight_spec],
                    out_specs=[whole(sums_shape.shape), whole(top_shape.shape)],
                ),
                compiler_params=roomy,
                cost_estimate=logits_cost,
            )(core_scalar, normed, weight)

        critic_sums, critic_top = head(critic_weight)
        policy_sums, policy_top = head(policy_weight)
        extra_in = [critic_sums, policy_sums, value_lanes, critic_top, policy_top, info]
        out_shape = [
            jax.ShapeDtypeStruct((tokens, 2 * width), f32),
            jax.ShapeDtypeStruct((mp_size, 8, tokens), f32),
            jax.ShapeDtypeStruct((8, tokens), f32),
        ]
        powers, totals, own_rows = pl.pallas_call(
            totals_kernel,
            out_shape=out_shape,
            grid_spec=pltpu.PrefetchScalarGridSpec(
                num_scalar_prefetch=2,
                grid=(CHUNKS,),
                in_specs=state_specs
                + [weight_spec] * 2
                + [whole(array.shape) for array in extra_in],
                out_specs=[whole(shape.shape) for shape in out_shape],
                scratch_shapes=[
                    pltpu.VMEM((tokens, LANES), f32),
                    pltpu.VMEM((1, width), f32),
                    pltpu.VMEM((tokens, CHUNK), bf16),
                    pltpu.VMEM((tokens, LANES), f32),
                ],
            ),
            compiler_params=roomy,
            cost_estimate=logits_cost,
        )(
            far_scalar,
            block_scalar,
            other,
            other,
            gain_row,
            value_row,
            critic_weight,
            policy_weight,
            *extra_in,
        )

    with jax.named_scope("totals"):
        totals, tile_is_row, share_is_row = lax.optimization_barrier(
            (totals, tile_is_row, share_is_row)
        )
        totals = lax.all_to_all(totals, "mp", 0, 0)
        totals = pl.pallas_call(
            merge_kernel,
            out_shape=jax.ShapeDtypeStruct((dp_size, 8, tokens), f32),
            compiler_params=roomy,
        )(totals)
        totals = lax.all_to_all(totals, "dp", 0, 0)

    matmul_cost = pl.CostEstimate(
        flops=2 * tokens * HALF * 2 * width,
        bytes_accessed=2 * (2 * HALF * width + 2 * tokens * HALF),
        transcendentals=0,
    )
    part_shape = (dp_size, TILES + TILES // rows, rows, LANES)

    def part(which, states, extra, with_grads):
        def chunk(i):
            return jnp.minimum(i, CHUNKS - 1)

        weight_spec = pl.BlockSpec(
            (CHUNK, width), lambda i, half, _: (half_of(half) * CHUNKS + chunk(i), 0)
        )
        out_shape = [jax.ShapeDtypeStruct(part_shape, f32)]
        out_specs = [pl.BlockSpec(state_block, lambda i, *_: (0, i, 0, 0))]
        if with_grads:
            out_shape += [
                jax.ShapeDtypeStruct((tokens, 2 * width), bf16),
                jax.ShapeDtypeStruct((tokens, LANES), f32),
            ]
            out_specs += [whole((tokens, 2 * width)), whole((tokens, LANES))]
        return pl.pallas_call(
            functools.partial(part_kernel, with_grads),
            out_shape=out_shape,
            grid_spec=pltpu.PrefetchScalarGridSpec(
                num_scalar_prefetch=2,
                grid=(CHUNKS + 1,),
                in_specs=[whole(array.shape) for array in extra]
                + [
                    pl.BlockSpec(state_block, lambda i, *_: (0, chunk(i), 0, 0)),
                    inverse_spec,
                    weight_spec,
                    weight_spec,
                ],
                out_specs=out_specs,
                scratch_shapes=[pltpu.VMEM((TILES, LANES), f32)]
                + [pltpu.VMEM((tokens, LANES), f32)] * 2,
            ),
            compiler_params=roomy,
            cost_estimate=matmul_cost,
        )(which, block_scalar, *extra, states, states, critic_weight, policy_weight)

    with jax.named_scope("reduce"):
        part_other, grads, column = part(
            far_scalar, other, [totals, own_rows, info, powers], True
        )
        arrived = swap(part_other.astype(f16))
        (part_mine,) = part(core_scalar, mine, [grads, column], False)
        joined = (part_mine + arrived.astype(f32)).astype(f16)
        lines = exchange(joined.reshape((side, side) + part_shape[1:]), False)

    def weight_grads(which, states, grads, earlier):
        far = bool(earlier)
        out_shape = [
            jax.ShapeDtypeStruct((D, width), bf16),
            jax.ShapeDtypeStruct((1, D), f32),
        ]
        out_specs = [
            pl.BlockSpec((CHUNK, width), lambda i, half: (half_of(half) * CHUNKS + i, 0)),
            pl.BlockSpec((1, CHUNK), lambda i, half: (0, half_of(half) * CHUNKS + i)),
        ]
        if not far:
            out_shape += [jax.ShapeDtypeStruct((TILES, LANES), f32)]
            out_specs += [pl.BlockSpec((CHUNK_TILES, LANES), lambda i, half: (i, 0))]
        return pl.pallas_call(
            functools.partial(weights_kernel, far),
            out_shape=out_shape,
            grid_spec=pltpu.PrefetchScalarGridSpec(
                num_scalar_prefetch=1,
                grid=(CHUNKS,),
                in_specs=[
                    pl.BlockSpec(state_block, lambda i, half: (0, i, 0, 0)),
                    inverse_spec,
                    pl.BlockSpec((1, CHUNK), lambda i, half: (0, half_of(half) * CHUNKS + i)),
                    pl.BlockSpec((tokens, width), lambda i, half: (0, 0)),
                    whole((tokens, LANES)),
                ]
                + [pl.BlockSpec(memory_space=pl.ANY)] * len(earlier),
                out_specs=out_specs,
                scratch_shapes=[pltpu.VMEM((tokens, CHUNK), bf16)]
                + [pltpu.VMEM((tokens, LANES), f32)] * 2,
            ),
            input_output_aliases={6: 0, 7: 1} if far else {},
            compiler_params=roomy,
            cost_estimate=pl.CostEstimate(
                flops=2 * tokens * HALF * width,
                bytes_accessed=2 * (HALF * width + 2 * tokens * HALF),
                transcendentals=0,
            ),
        )(which, states, states, gain_row, grads, column, *earlier)

    with jax.named_scope("lines"):
        lines, grads = lax.optimization_barrier((lines, grads))
        line = pack(jnp.sum(lines.astype(f32), axis=0), tile_is_row)
        parts = exchange(line, True)
        grad_critic, grad_value, extra = weight_grads(core_scalar, mine, grads, [])
        token = lax.dynamic_slice(column, (block_index, 0), (1, LANES))
        state_row = lax.dynamic_slice_in_dim(hidden_state, mp_index, 1, 0).reshape(
            2 * TILES, LANES
        )
        parts, grads, extra, token, state_row = lax.optimization_barrier(
            (parts, grads, extra, token, state_row)
        )

    with jax.named_scope("chips"):
        block = jnp.sum(unpack(parts, tile_is_row), axis=0).reshape(-1, LANES)
        shares = pl.pallas_call(
            split_kernel,
            out_shape=jax.ShapeDtypeStruct((chip_count, 3 * TILES, LANES), f32),
            compiler_params=roomy,
        )(block)
        shares = lax.all_to_all(
            pack(shares, share_is_row), "mp", 0, 0, axis_index_groups=chip_groups
        )
        far_extra = swap(extra)
        grad_critic, grad_value = weight_grads(
            far_scalar, other, grads, [grad_critic, grad_value]
        )
        shares, far_extra, grad_value = lax.optimization_barrier((shares, far_extra, grad_value))
        own = jnp.sum(unpack(shares, share_is_row), axis=0)
        far = swap(own)

    with jax.named_scope("finish"):
        smem = pl.BlockSpec(memory_space=pltpu.SMEM)
        vmem = pl.BlockSpec(memory_space=pltpu.VMEM)
        grad_hidden, grad_gain = pl.pallas_call(
            finish_kernel,
            out_shape=[
                jax.ShapeDtypeStruct((1, D), bf16),
                jax.ShapeDtypeStruct((2 * TILES, LANES), f32),
            ],
            in_specs=[smem] + [vmem] * 8,
            compiler_params=roomy,
        )(
            core_scalar,
            token,
            own,
            far,
            extra,
            far_extra,
            state_row,
            norm_gain.reshape(2 * TILES, LANES),
            value_weight.reshape(2 * TILES, LANES),
        )
    return (grad_hidden, grad_gain.reshape(D), grad_critic, grad_value.reshape(D))


def solution(mesh):
    placed = (
        P("dp", None),
        P(),
        P(None, ("dp", "mp")),
        P(None, ("dp", "mp")),
        P(),
        P(),
        P(),
        P(),
        P(),
    )
    return jax.shard_map(
        body,
        mesh=mesh,
        in_specs=placed,
        out_specs=(P(("dp", "mp"), None), P(), P(None, ("dp", "mp")), P()),
        check_vma=False,
    )
```
